32 devices in a mesh: grp: 4 (over y, x), band: 8 (over z, core).
Axes of the slice: x: 2, y: 2, z: 4, core: 2. Of those that a mesh axis runs over, the one named last changes fastest.
Arguments:
- orbitals: bfloat16 [32, 64, 4096], P('band'), may hold values from -6 to 6
Outputs:
- exchange: float32 [32, 64, 4096], P('band', 'grp')
The draws below stay inside these ranges and needn't reach their ends.
All inputs are finite; a program needn't handle non-finite values.
Results may differ from the reference program's by a relative error of at most 0.0003.
Values may be sent and summed in bfloat16 or wider, within the bound.
A program may use at most 128 MiB of HBM per device.

```python
import math
import jax
import jax.numpy as jnp
from jax import lax

GRID = 64
OWN = 4
ROUNDS = 2
BANDS = 32
N_BAND = 8


def level_of(key, shape, split, low, largest):
    def one(axis_at, shards_of):
        draws = jax.random.uniform(jax.random.fold_in(jax.random.fold_in(key, 6), axis_at), (shards_of,), jnp.float32, low / len(split), largest / len(split))
        return jnp.repeat(jnp.exp(draws), shape[axis_at] // shards_of).reshape((-1,) + (1,) * (len(shape) - axis_at - 1))

    loudness = one(*split[0])
    for cut in split[1:]:
        loudness = loudness * one(*cut)
    return loudness


def scatter_about(own_key, dims, scale, bound, shards=(), held_as=jnp.bfloat16):
    drawn = jax.random.normal(own_key, dims, jnp.float32) * scale
    if len(shards) > 0:
        drawn = level_of(own_key, dims, shards, -0.22, 0.18) * drawn
    return jnp.clip(drawn, min=-bound, max=bound).astype(held_as)


def setup_inputs(seed: int = 0) -> dict:
    key_of = jax.random.split(jax.random.key(seed), 2)
    return {
        "orbitals": scatter_about(key_of[0], (BANDS, GRID, GRID * GRID), 1.0, 6.0, ((0, 8),)),
    }


CELL_LENGTH = 41.05
SCREENING = 0.106


def kernel_table(grid):
    wavenum = jnp.arange(grid, dtype=jnp.int32)
    wavenum = jnp.where(wavenum < grid // 2, wavenum, wavenum - grid).astype(jnp.float32) * (2.0 * math.pi / CELL_LENGTH)
    squared = wavenum[:, None, None] ** 2 + wavenum[None, :, None] ** 2 + wavenum[None, None, :] ** 2
    safe = jnp.where(squared > 0, squared, 1.0)
    screened = 4.0 * math.pi * (1.0 - jnp.exp(-safe / (4.0 * SCREENING * SCREENING))) / safe
    return jnp.where(squared > 0, screened, math.pi / (SCREENING * SCREENING)).astype(jnp.float32)


def reference(orbitals):
    fields = orbitals.astype(jnp.float32).reshape(BANDS, GRID, GRID, GRID)
    kernel = kernel_table(GRID)
    distances = jnp.array([d for r in range(1, ROUNDS + 1) for d in (r, -r)], dtype=jnp.int32)
    members = jnp.arange(OWN, dtype=jnp.int32)

    def exchange_band(band_index):
        block = band_index // OWN
        partners = (((block + distances[:, None]) % N_BAND) * OWN + members[None, :]).reshape(-1)
        partner_fields = fields[partners]
        density = fields[band_index][None] * partner_fields
        spectrum = jnp.fft.fftn(density, axes=(1, 2, 3)) * kernel
        potential = jnp.real(jnp.fft.ifftn(spectrum, axes=(1, 2, 3)))
        return -0.25 * jnp.sum(partner_fields * potential, axis=0)

    result = lax.map(exchange_band, jnp.arange(BANDS, dtype=jnp.int32))
    return result.reshape(BANDS, GRID, GRID * GRID)
```

```python
import functools
import math

import jax
import jax.numpy as jnp
import ml_dtypes
import numpy as np
from jax import lax
from jax.experimental import pallas as pl
from jax.experimental.pallas import tpu as pltpu
from jax.sharding import PartitionSpec as P

ROUNDS = 2


CELL_LENGTH = 41.05
SCREENING = 0.106
LANES = 128


def from_behind(shard, axis, by):
    count = lax.axis_size(axis)
    return lax.ppermute(shard, axis, [(i, (i + by) % count) for i in range(count)])


def kernel_table(grid):
    wavenum = np.arange(grid, dtype=np.float64)
    wavenum = np.where(wavenum < grid // 2, wavenum, wavenum - grid) * (2.0 * math.pi / CELL_LENGTH)
    squared = (
        wavenum[:, None, None] ** 2 + wavenum[None, :, None] ** 2 + wavenum[None, None, :] ** 2
    )
    safe = np.where(squared > 0, squared, 1.0)
    screened = 4.0 * math.pi * (1.0 - np.exp(-safe / (4.0 * SCREENING * SCREENING))) / safe
    return np.where(squared > 0, screened, math.pi / (SCREENING * SCREENING))


def tables(grid, copies):
    indices = np.arange(grid)
    angles = (indices[:, None] * indices[None, :] % grid) * (2.0 * math.pi / grid)
    wide = np.kron(np.eye(copies), np.cos(angles) + np.sin(angles))
    high = wide.astype(ml_dtypes.bfloat16)
    low = (wide - high.astype(np.float64)).astype(ml_dtypes.bfloat16)
    return np.concatenate([high, high, low], axis=1)


def parts_of(values, axis):
    high = values.astype(jnp.bfloat16)
    low = (values - high.astype(jnp.float32)).astype(jnp.bfloat16)
    return jnp.concatenate([high, low, high], axis=axis)


def dot(a, b, dims=((1,), (0,))):
    return lax.dot_general(a, b, (dims, ((), ())), preferred_element_type=jnp.float32)


def pair_kernel(grid, step, own_ref, visit_ref, table_ref, right_ref, wide_ref, slim_ref, *rest):
    if len(rest) == 5:
        before_ref, home_ref, back_ref, t_ref, u_ref = rest
    else:
        before_ref = None
        home_ref, back_ref, t_ref, u_ref = rest
    count, _, plane = own_ref.shape
    width = count * grid
    lines = step // grid
    halves = width // LANES

    def forward(c, _):
        lanes = pl.ds(pl.multiple_of(c * step, step), step)
        visit = visit_ref[:, lanes].astype(jnp.float32)
        density = jnp.concatenate(
            [own_ref[n, :, lanes].astype(jnp.float32) * visit for n in range(count)], axis=0
        )
        turned = dot(parts_of(density.T, 1), right_ref[...], ((1,), (1,)))
        turned = dot(wide_ref[...], parts_of(turned, 0))
        for j in range(lines):
            for h in range(halves):
                t_ref[h, pl.ds(c * lines + j, grid, stride=grid), :] = turned[
                    j * grid : (j + 1) * grid, h * LANES : (h + 1) * LANES
                ]
        return 0

    lax.fori_loop(0, plane // step, forward, 0)

    def middle(k, _):
        for j in range(lines):
            row = k * lines + j
            rows = pl.ds(pl.multiple_of(row * grid, grid), grid)
            values = jnp.concatenate([t_ref[h, rows, :] for h in range(halves)], axis=1)
            scale = jnp.concatenate([table_ref[rows, :]] * halves, axis=1)
            values = dot(slim_ref[...], parts_of(values, 0)) * scale
            values = dot(slim_ref[...], parts_of(values, 0))
            for h in range(halves):
                u_ref[h, pl.ds(row, grid, stride=grid), :] = values[:, h * LANES : (h + 1) * LANES]
        return 0

    lax.fori_loop(0, grid // lines, middle, 0)

    def backward(c, _):
        lanes = pl.ds(pl.multiple_of(c * step, step), step)
        values = jnp.concatenate([u_ref[h, lanes, :] for h in range(halves)], axis=1)
        values = dot(wide_ref[...], parts_of(values, 0))
        potential = dot(right_ref[...], parts_of(values, 1), ((1,), (1,)))
        visit = visit_ref[:, lanes].astype(jnp.float32)
        total = None
        for n in range(count):
            one = potential[n * grid : (n + 1) * grid, :]
            term = visit * one
            if before_ref is not None:
                term = term + before_ref[n, :, lanes]
            home_ref[n, :, lanes] = term
            term = own_ref[n, :, lanes].astype(jnp.float32) * one
            total = term if total is None else total + term
        back_ref[:, lanes] = total
        return 0

    lax.fori_loop(0, plane // step, backward, 0)


def pairs(own, visit, before, consts):
    count, grid, plane = own.shape
    step = 4 * grid
    width = count * grid
    extra = () if before is None else (before,)
    vmem = pl.BlockSpec(memory_space=pltpu.VMEM)
    return pl.pallas_call(
        functools.partial(pair_kernel, grid, step),
        out_shape=(
            jax.ShapeDtypeStruct((count, grid, plane), jnp.float32),
            jax.ShapeDtypeStruct((grid, plane), jnp.float32),
        ),
        in_specs=[vmem] * (6 + len(extra)),
        out_specs=(vmem, vmem),
        scratch_shapes=[
            pltpu.VMEM((width // LANES, grid * grid, LANES), jnp.float32),
            pltpu.VMEM((width // LANES, grid * grid, LANES), jnp.float32),
        ],
        cost_estimate=pl.CostEstimate(
            flops=36 * plane * width * step, bytes_accessed=16 * count * grid * plane, transcendentals=0
        ),
        compiler_params=pltpu.CompilerParams(vmem_limit_bytes=48 * 1024 * 1024),
    )(own, visit, *consts, *extra)


def body(orbitals):
    own_count, grid, plane = orbitals.shape
    groups = lax.axis_size("grp")
    split_count = groups // own_count
    count = own_count // split_count
    group_index = lax.axis_index("grp")
    band_row = group_index // split_count
    own_start = group_index % split_count * count
    own = orbitals if count == own_count else lax.dynamic_slice_in_dim(orbitals, own_start, count, 0)
    outgoing = lax.dynamic_index_in_dim(orbitals, band_row, 0, keepdims=False)
    table = kernel_table(grid).reshape(grid * grid, grid) * (-0.25 / float(grid**3))
    consts = (
        jnp.asarray(np.tile(table, (1, LANES // grid)).astype(np.float32)),
        jnp.asarray(tables(grid, count)),
        jnp.asarray(tables(grid, 4)),
        jnp.asarray(tables(grid, 1)),
    )
    home = None
    returned = None
    arrivals = [from_behind(outgoing, "band", d) for d in range(1, ROUNDS + 1)]
    for distance in range(1, ROUNDS + 1):
        home, back = pairs(own, arrivals[distance - 1], home, consts)
        back = from_behind(back, "band", -distance)
        returned = back if returned is None else returned + back
    zeros = jnp.zeros((own_count, grid, plane), jnp.float32)
    buffer = home if count == own_count else lax.dynamic_update_slice(zeros, home, (own_start, 0, 0))
    mine = jnp.arange(own_count)[:, None, None] == band_row
    buffer = buffer + jnp.where(mine, returned[None], 0.0)
    return lax.psum_scatter(buffer, "grp", scatter_dimension=1, tiled=True)


def solution(mesh):
    return jax.shard_map(
        body,
        mesh=mesh,
        in_specs=(P("band", None, None),),
        out_specs=P("band", "grp", None),
        check_vma=False,
    )
```

```python
import functools
import math

import jax
import jax.numpy as jnp
import ml_dtypes
import numpy as np
from jax import lax
from jax.experimental import pallas as pl
from jax.experimental.pallas import tpu as pltpu
from jax.sharding import PartitionSpec as P

ROUNDS = 2


CELL_LENGTH = 41.05
SCREENING = 0.106
LANES = 128
PARTS = 2
MESH = pl.DeviceIdType.MESH


def kernel_table(grid):
    wavenum = np.arange(grid, dtype=np.float64)
    wavenum = np.where(wavenum < grid // 2, wavenum, wavenum - grid) * (2.0 * math.pi / CELL_LENGTH)
    squared = (
        wavenum[:, None, None] ** 2 + wavenum[None, :, None] ** 2 + wavenum[None, None, :] ** 2
    )
    safe = np.where(squared > 0, squared, 1.0)
    screened = 4.0 * math.pi * (1.0 - np.exp(-safe / (4.0 * SCREENING * SCREENING))) / safe
    return np.where(squared > 0, screened, math.pi / (SCREENING * SCREENING))


def tables(grid, copies):
    indices = np.arange(grid)
    angles = (indices[:, None] * indices[None, :] % grid) * (2.0 * math.pi / grid)
    wide = np.kron(np.eye(copies), np.cos(angles) + np.sin(angles))
    high = wide.astype(ml_dtypes.bfloat16)
    low = (wide - high.astype(np.float64)).astype(ml_dtypes.bfloat16)
    return np.concatenate([high, high, low], axis=1)


def parts_of(values, axis):
    high = values.astype(jnp.bfloat16)
    low = (values - high.astype(jnp.float32)).astype(jnp.bfloat16)
    return jnp.concatenate([high, low, high], axis=axis)


def dot(a, b, dims=((1,), (0,))):
    return lax.dot_general(a, b, (dims, ((), ())), preferred_element_type=jnp.float32)


def exchange_kernel(
    grid,
    step,
    groups,
    ring,
    orbitals_ref,
    table_ref,
    right_ref,
    wide_ref,
    slim_ref,
    out_ref,
    visit_ref,
    home_ref,
    back_ref,
    home_got,
    back_got,
    t_ref,
    u_ref,
    in_send,
    in_recv,
    home_send,
    home_recv,
    back_send,
    back_recv,
):
    own_count, _, plane = orbitals_ref.shape
    split_count = groups // own_count
    count = own_count // split_count
    planes = grid // groups
    width = count * grid
    lines = step // grid
    halves = width // LANES
    part = plane // PARTS
    group, band = lax.axis_index("grp"), lax.axis_index("band")
    band_row = group // split_count
    own_start = lax.rem(group, split_count) * count

    def device(by, along):
        return (lax.rem(group + by, groups), lax.rem(band + along + ring, ring))

    barrier = pltpu.get_barrier_semaphore()
    greeted = 0
    for along in range(-ROUNDS, ROUNDS + 1):
        for by in range(groups):
            if by or along:
                pl.semaphore_signal(
                    barrier, inc=1, device_id=device(by, along), device_id_type=MESH
                )
                greeted += 1
    pl.semaphore_wait(barrier, greeted)

    def remote(source, target, send, recv, where):
        copy = pltpu.make_async_remote_copy(
            src_ref=source,
            dst_ref=target,
            send_sem=send,
            recv_sem=recv,
            device_id=where,
            device_id_type=MESH,
        )
        copy.start()
        return copy

    def lanes_of(p):
        return pl.ds(p * part, part)

    def rows_of(by):
        return pl.ds(pl.multiple_of(lax.rem(group + by, groups) * planes, planes), planes)

    arrivals = [
        [
            remote(
                orbitals_ref.at[band_row, :, lanes_of(p)],
                visit_ref.at[d, :, lanes_of(p)],
                in_send.at[d, p],
                in_recv.at[d, p],
                device(0, d + 1),
            )
            for p in range(PARTS)
        ]
        for d in range(ROUNDS)
    ]

    def own_of(n, lanes):
        return orbitals_ref[own_start + n, :, lanes].astype(jnp.float32)

    def forward(d, c, _):
        lanes = pl.ds(pl.multiple_of(c * step, step), step)
        visit = visit_ref[d, :, lanes].astype(jnp.float32)
        density = jnp.concatenate([own_of(n, lanes) * visit for n in range(count)], axis=0)
        turned = dot(parts_of(density.T, 1), right_ref[...], ((1,), (1,)))
        turned = dot(wide_ref[...], parts_of(turned, 0))
        for j in range(lines):
            for h in range(halves):
                t_ref[h, pl.ds(c * lines + j, grid, stride=grid), :] = turned[
                    j * grid : (j + 1) * grid, h * LANES : (h + 1) * LANES
                ]
        return 0

    def middle(k, _):
        for j in range(lines):
            row = k * lines + j
            rows = pl.ds(pl.multiple_of(row * grid, grid), grid)
            values = jnp.concatenate([t_ref[h, rows, :] for h in range(halves)], axis=1)
            scale = jnp.concatenate([table_ref[rows, :]] * halves, axis=1)
            values = dot(slim_ref[...], parts_of(values, 0)) * scale
            values = dot(slim_ref[...], parts_of(values, 0))
            for h in range(halves):
                u_ref[h, pl.ds(row, grid, stride=grid), :] = values[:, h * LANES : (h + 1) * LANES]
        return 0

    def backward(d, c, _):
        lanes = pl.ds(pl.multiple_of(c * step, step), step)
        values = jnp.concatenate([u_ref[h, lanes, :] for h in range(halves)], axis=1)
        values = dot(wide_ref[...], parts_of(values, 0))
        potential = dot(right_ref[...], parts_of(values, 1), ((1,), (1,)))
        visit = visit_ref[d, :, lanes].astype(jnp.float32)
        total = None
        for n in range(count):
            one = potential[n * grid : (n + 1) * grid, :]
            term = visit * one
            if d > 0:
                term = term + home_ref[n, :, lanes]
            home_ref[n, :, lanes] = term
            term = own_of(n, lanes) * one
            total = term if total is None else total + term
        back_ref[d, :, lanes] = total
        return 0

    chunks = part // step
    home_copies = [[] for _ in range(PARTS)]
    back_copies = [[[] for _ in range(PARTS)] for _ in range(ROUNDS)]
    for d in range(ROUNDS):
        for p in range(PARTS):
            arrivals[d][p].wait_recv()
            lax.fori_loop(p * chunks, (p + 1) * chunks, functools.partial(forward, d), 0)
        lax.fori_loop(0, grid // lines, middle, 0)
        for p in range(PARTS):
            lax.fori_loop(p * chunks, (p + 1) * chunks, functools.partial(backward, d), 0)
            lanes = lanes_of(p)
            for by in range(groups):
                back_copies[d][p].append(
                    remote(
                        back_ref.at[d, rows_of(by), lanes],
                        back_got.at[d, by, :, lanes],
                        back_send.at[d, by, p],
                        back_recv.at[d, by, p],
                        device(by, -d - 1),
                    )
                )
            if d == ROUNDS - 1:
                for by in range(1, groups):
                    home_copies[p].append(
                        remote(
                            home_ref.at[:, rows_of(by), lanes],
                            home_got.at[by - 1, :, :, lanes],
                            home_send.at[by - 1, p],
                            home_recv.at[by - 1, p],
                            device(by, 0),
                        )
                    )

    if count < own_count:
        out_ref[...] = jnp.zeros_like(out_ref)
    out_ref[pl.ds(own_start, count)] = home_ref[:, rows_of(0), :]
    for d in range(ROUNDS):
        for p in range(PARTS):
            lanes = lanes_of(p)
            if d == ROUNDS - 1:
                for by in range(1, groups):
                    home_copies[p][by - 1].wait_recv()
                    source = lax.rem(group + groups - by, groups)
                    start = lax.rem(source, split_count) * count
                    out_ref[pl.ds(start, count), :, lanes] += home_got[by - 1, :, :, lanes]
            for by in range(groups):
                back_copies[d][p][by].wait_recv()
                row = lax.rem(group + groups - by, groups) // split_count
                out_ref[row, :, lanes] += back_got[d, by, :, lanes]
    for p in range(PARTS):
        for copy in home_copies[p]:
            copy.wait_send()
        for d in range(ROUNDS):
            arrivals[d][p].wait_send()
            for copy in back_copies[d][p]:
                copy.wait_send()


def body(orbitals):
    own_count, grid, plane = orbitals.shape
    groups, ring = lax.axis_size("grp"), lax.axis_size("band")
    count = own_count // (groups // own_count)
    planes = grid // groups
    width = count * grid
    step = 4 * grid
    table = kernel_table(grid).reshape(grid * grid, grid) * (-0.25 / float(grid**3))
    consts = (
        jnp.asarray(np.tile(table, (1, LANES // grid)).astype(np.float32)),
        jnp.asarray(tables(grid, count)),
        jnp.asarray(tables(grid, 4)),
        jnp.asarray(tables(grid, 1)),
    )
    vmem = pl.BlockSpec(memory_space=pltpu.VMEM)
    dma = pltpu.SemaphoreType.DMA
    return pl.pallas_call(
        functools.partial(exchange_kernel, grid, step, groups, ring),
        out_shape=jax.ShapeDtypeStruct((own_count, planes, plane), jnp.float32),
        in_specs=[vmem] * 5,
        out_specs=vmem,
        scratch_shapes=[
            pltpu.VMEM((ROUNDS, grid, plane), jnp.bfloat16),
            pltpu.VMEM((count, grid, plane), jnp.float32),
            pltpu.VMEM((ROUNDS, grid, plane), jnp.float32),
            pltpu.VMEM((groups - 1, count, planes, plane), jnp.float32),
            pltpu.VMEM((ROUNDS, groups, planes, plane), jnp.float32),
            pltpu.VMEM((width // LANES, grid * grid, LANES), jnp.float32),
            pltpu.VMEM((width // LANES, grid * grid, LANES), jnp.float32),
            dma((ROUNDS, PARTS)),
            dma((ROUNDS, PARTS)),
            dma((groups - 1, PARTS)),
            dma((groups - 1, PARTS)),
            dma((ROUNDS, groups, PARTS)),
            dma((ROUNDS, groups, PARTS)),
        ],
        compiler_params=pltpu.CompilerParams(
            collective_id=0, has_side_effects=True, vmem_limit_bytes=48 * 1024 * 1024
        ),
    )(orbitals, *consts)


def solution(mesh):
    return jax.shard_map(
        body,
        mesh=mesh,
        in_specs=(P("band", None, None),),
        out_specs=P("band", "grp", None),
        check_vma=False,
    )
```

```python
import functools
import math

import jax
import jax.numpy as jnp
import ml_dtypes
import numpy as np
from jax import lax
from jax.experimental import pallas as pl
from jax.experimental.pallas import tpu as pltpu
from jax.sharding import PartitionSpec as P

ROUNDS = 2


CELL_LENGTH = 41.05
SCREENING = 0.106
LANES = 128
PARTS = 4
UNROLL = 4
MESH = pl.DeviceIdType.MESH


def kernel_table(grid):
    wavenum = np.arange(grid, dtype=np.float64)
    wavenum = np.where(wavenum < grid // 2, wavenum, wavenum - grid) * (2.0 * math.pi / CELL_LENGTH)
    squared = (
        wavenum[:, None, None] ** 2 + wavenum[None, :, None] ** 2 + wavenum[None, None, :] ** 2
    )
    safe = np.where(squared > 0, squared, 1.0)
    screened = 4.0 * math.pi * (1.0 - np.exp(-safe / (4.0 * SCREENING * SCREENING))) / safe
    return np.where(squared > 0, screened, math.pi / (SCREENING * SCREENING))


def tables(grid, copies):
    indices = np.arange(grid)
    angles = (indices[:, None] * indices[None, :] % grid) * (2.0 * math.pi / grid)
    wide = np.kron(np.eye(copies), np.cos(angles) + np.sin(angles))
    high = wide.astype(ml_dtypes.bfloat16)
    low = (wide - high.astype(np.float64)).astype(ml_dtypes.bfloat16)
    return np.concatenate([high, high, low], axis=1)


def parts_of(values, axis):
    high = values.astype(jnp.bfloat16)
    low = (values - high.astype(jnp.float32)).astype(jnp.bfloat16)
    return jnp.concatenate([high, low, high], axis=axis)


def dot(a, b, dims=((1,), (0,))):
    return lax.dot_general(a, b, (dims, ((), ())), preferred_element_type=jnp.float32)


def exchange_kernel(
    grid,
    step,
    groups,
    ring,
    orbitals_ref,
    table_hbm,
    right_hbm,
    slim_hbm,
    out_ref,
    own_ref,
    table_ref,
    right_ref,
    slim_ref,
    visit_ref,
    home_ref,
    back_ref,
    home_got,
    back_got,
    t_ref,
    u_ref,
    local_sem,
    in_send,
    in_recv,
    home_send,
    home_recv,
    back_send,
    back_recv,
):
    own_count, _, plane = orbitals_ref.shape
    split_count = groups // own_count
    count = own_count // split_count
    planes = grid // groups
    width = count * grid
    lines = step // grid
    halves = width // LANES
    part = plane // PARTS
    group, band = lax.axis_index("grp"), lax.axis_index("band")
    band_row = group // split_count
    own_start = lax.rem(group, split_count) * count

    def device(by, along):
        return (lax.rem(group + by, groups), lax.rem(band + along + ring, ring))

    locals_ = [
        pltpu.make_async_copy(orbitals_ref.at[pl.ds(own_start, count)], own_ref, local_sem.at[0]),
        pltpu.make_async_copy(right_hbm, right_ref, local_sem.at[1]),
        pltpu.make_async_copy(slim_hbm, slim_ref, local_sem.at[2]),
        pltpu.make_async_copy(table_hbm, table_ref, local_sem.at[3]),
    ]
    for copy in locals_:
        copy.start()

    barrier = pltpu.get_barrier_semaphore()
    greeted = 0
    for along in range(-ROUNDS, ROUNDS + 1):
        for by in range(groups):
            if by or along:
                pl.semaphore_signal(
                    barrier, inc=1, device_id=device(by, along), device_id_type=MESH
                )
                greeted += 1
    pl.semaphore_wait(barrier, greeted)

    def remote(source, target, send, recv, where):
        copy = pltpu.make_async_remote_copy(
            src_ref=source,
            dst_ref=target,
            send_sem=send,
            recv_sem=recv,
            device_id=where,
            device_id_type=MESH,
        )
        copy.start()
        return copy

    def lanes_of(p):
        return pl.ds(p * part, part)

    def rows_of(by):
        return pl.ds(pl.multiple_of(lax.rem(group + by, groups) * planes, planes), planes)

    arrivals = [
        [
            remote(
                orbitals_ref.at[band_row, :, lanes_of(p)],
                visit_ref.at[d, :, lanes_of(p)],
                in_send.at[d, p],
                in_recv.at[d, p],
                device(0, d + 1),
            )
            for p in range(PARTS)
        ]
        for d in range(ROUNDS)
    ]

    def own_of(n, lanes):
        return own_ref[n, :, lanes].astype(jnp.float32)

    def slim_lines(values):
        return jnp.concatenate(
            [
                dot(slim_ref[...], parts_of(values[j * grid : (j + 1) * grid], 0))
                for j in range(lines)
            ],
            axis=0,
        )

    def forward(d, c, _):
        lanes = pl.ds(pl.multiple_of(c * step, step), step)
        visit = visit_ref[d, :, lanes].astype(jnp.float32)
        density = jnp.concatenate([own_of(n, lanes) * visit for n in range(count)], axis=0)
        turned = dot(parts_of(density.T, 1), right_ref[...], ((1,), (1,)))
        turned = slim_lines(turned)
        for j in range(lines):
            for h in range(halves):
                t_ref[h, pl.ds(c * lines + j, grid, stride=grid), :] = turned[
                    j * grid : (j + 1) * grid, h * LANES : (h + 1) * LANES
                ]
        return 0

    def middle(k, _):
        for j in range(lines):
            row = k * lines + j
            rows = pl.ds(pl.multiple_of(row * grid, grid), grid)
            values = jnp.concatenate([t_ref[h, rows, :] for h in range(halves)], axis=1)
            scale = jnp.concatenate([table_ref[rows, :]] * halves, axis=1)
            values = dot(slim_ref[...], parts_of(values, 0)) * scale
            values = dot(slim_ref[...], parts_of(values, 0))
            for h in range(halves):
                u_ref[h, pl.ds(row, grid, stride=grid), :] = values[:, h * LANES : (h + 1) * LANES]
        return 0

    def backward(d, c, _):
        lanes = pl.ds(pl.multiple_of(c * step, step), step)
        values = jnp.concatenate([u_ref[h, lanes, :] for h in range(halves)], axis=1)
        values = slim_lines(values)
        potential = dot(right_ref[...], parts_of(values, 1), ((1,), (1,)))
        visit = visit_ref[d, :, lanes].astype(jnp.float32)
        total = None
        for n in range(count):
            one = potential[n * grid : (n + 1) * grid, :]
            term = visit * one
            if d > 0:
                term = term + home_ref[n, :, lanes]
            home_ref[n, :, lanes] = term
            term = own_of(n, lanes) * one
            total = term if total is None else total + term
        back_ref[d, :, lanes] = total
        return 0

    chunks = part // step
    home_copies = [[] for _ in range(PARTS)]
    back_copies = [[[] for _ in range(PARTS)] for _ in range(ROUNDS)]
    for copy in locals_:
        copy.wait()
    for d in range(ROUNDS):
        for p in range(PARTS):
            arrivals[d][p].wait_recv()
            lax.fori_loop(p * chunks, (p + 1) * chunks, functools.partial(forward, d), 0, unroll=UNROLL)
        lax.fori_loop(0, grid // lines, middle, 0, unroll=UNROLL)
        for p in range(PARTS):
            lax.fori_loop(p * chunks, (p + 1) * chunks, functools.partial(backward, d), 0, unroll=UNROLL)
            lanes = lanes_of(p)
            for by in range(groups):
                back_copies[d][p].append(
                    remote(
                        back_ref.at[d, rows_of(by), lanes],
                        back_got.at[d, by, :, lanes],
                        back_send.at[d, by, p],
                        back_recv.at[d, by, p],
                        device(by, -d - 1),
                    )
                )
            if d == ROUNDS - 1:
                for by in range(1, groups):
                    home_copies[p].append(
                        remote(
                            home_ref.at[:, rows_of(by), lanes],
                            home_got.at[by - 1, :, :, lanes],
                            home_send.at[by - 1, p],
                            home_recv.at[by - 1, p],
                            device(by, 0),
                        )
                    )

    if count < own_count:
        out_ref[...] = jnp.zeros_like(out_ref)
    out_ref[pl.ds(own_start, count)] = home_ref[:, rows_of(0), :]
    for d in range(ROUNDS):
        for p in range(PARTS):
            lanes = lanes_of(p)
            if d == ROUNDS - 1:
                for by in range(1, groups):
                    home_copies[p][by - 1].wait_recv()
                    source = lax.rem(group + groups - by, groups)
                    start = lax.rem(source, split_count) * count
                    out_ref[pl.ds(start, count), :, lanes] += home_got[by - 1, :, :, lanes]
            for by in range(groups):
                back_copies[d][p][by].wait_recv()
                row = lax.rem(group + groups - by, groups) // split_count
                out_ref[row, :, lanes] += back_got[d, by, :, lanes]
    for p in range(PARTS):
        for copy in home_copies[p]:
            copy.wait_send()
        for d in range(ROUNDS):
            arrivals[d][p].wait_send()
            for copy in back_copies[d][p]:
                copy.wait_send()


def body(orbitals):
    own_count, grid, plane = orbitals.shape
    groups, ring = lax.axis_size("grp"), lax.axis_size("band")
    count = own_count // (groups // own_count)
    planes = grid // groups
    width = count * grid
    step = 4 * grid
    table = kernel_table(grid).reshape(grid * grid, grid) * (-0.25 / float(grid**3))
    consts = (
        jnp.asarray(np.tile(table, (1, LANES // grid)).astype(np.float32)),
        jnp.asarray(tables(grid, count)),
        jnp.asarray(tables(grid, 1)),
    )
    vmem = pl.BlockSpec(memory_space=pltpu.VMEM)
    dma = pltpu.SemaphoreType.DMA
    return pl.pallas_call(
        functools.partial(exchange_kernel, grid, step, groups, ring),
        out_shape=jax.ShapeDtypeStruct((own_count, planes, plane), jnp.float32),
        in_specs=[pl.BlockSpec(memory_space=pl.ANY)] * 4,
        out_specs=vmem,
        scratch_shapes=[
            pltpu.VMEM((count, grid, plane), jnp.bfloat16),
            *[pltpu.VMEM(c.shape, c.dtype) for c in consts],
            pltpu.VMEM((ROUNDS, grid, plane), jnp.bfloat16),
            pltpu.VMEM((count, grid, plane), jnp.float32),
            pltpu.VMEM((ROUNDS, grid, plane), jnp.float32),
            pltpu.VMEM((groups - 1, count, planes, plane), jnp.float32),
            pltpu.VMEM((ROUNDS, groups, planes, plane), jnp.float32),
            pltpu.VMEM((width // LANES, grid * grid, LANES), jnp.float32),
            pltpu.VMEM((width // LANES, grid * grid, LANES), jnp.float32),
            dma((4,)),
            dma((ROUNDS, PARTS)),
            dma((ROUNDS, PARTS)),
            dma((groups - 1, PARTS)),
            dma((groups - 1, PARTS)),
            dma((ROUNDS, groups, PARTS)),
            dma((ROUNDS, groups, PARTS)),
        ],
        compiler_params=pltpu.CompilerParams(
            collective_id=0, has_side_effects=True, vmem_limit_bytes=48 * 1024 * 1024
        ),
    )(orbitals, *consts)


def solution(mesh):
    return jax.shard_map(
        body,
        mesh=mesh,
        in_specs=(P("band", None, None),),
        out_specs=P("band", "grp", None),
        check_vma=False,
    )
```

```python
import functools
import math

import jax
import jax.numpy as jnp
import ml_dtypes
import numpy as np
from jax import lax
from jax.experimental import pallas as pl
from jax.experimental.pallas import tpu as pltpu
from jax.sharding import PartitionSpec as P

ROUNDS = 2


CELL_LENGTH = 41.05
SCREENING = 0.106
LANES = 128
PARTS = 4
UNROLL = 4
PAIRS = 4
MESH = pl.DeviceIdType.MESH


def kernel_table(grid):
    wavenum = np.arange(grid, dtype=np.float64)
    wavenum = np.where(wavenum < grid // 2, wavenum, wavenum - grid) * (2.0 * math.pi / CELL_LENGTH)
    squared = (
        wavenum[:, None, None] ** 2 + wavenum[None, :, None] ** 2 + wavenum[None, None, :] ** 2
    )
    safe = np.where(squared > 0, squared, 1.0)
    screened = 4.0 * math.pi * (1.0 - np.exp(-safe / (4.0 * SCREENING * SCREENING))) / safe
    return np.where(squared > 0, screened, math.pi / (SCREENING * SCREENING))


def tables(grid, copies):
    indices = np.arange(grid)
    angles = (indices[:, None] * indices[None, :] % grid) * (2.0 * math.pi / grid)
    wide = np.kron(np.eye(copies), np.cos(angles) + np.sin(angles))
    high = wide.astype(ml_dtypes.bfloat16)
    low = (wide - high.astype(np.float64)).astype(ml_dtypes.bfloat16)
    return np.concatenate([high, high, low], axis=1)


def parts_of(values, axis):
    high = values.astype(jnp.bfloat16)
    low = (values - high.astype(jnp.float32)).astype(jnp.bfloat16)
    return jnp.concatenate([high, low, high], axis=axis)


def dot(a, b, dims=((1,), (0,))):
    return lax.dot_general(a, b, (dims, ((), ())), preferred_element_type=jnp.float32)


def bands_per_set(count):
    return min(count, PAIRS // ROUNDS)


def exchange_kernel(
    grid,
    step,
    groups,
    ring,
    orbitals_ref,
    table_hbm,
    right_hbm,
    slim_hbm,
    out_ref,
    own_ref,
    table_ref,
    right_ref,
    slim_ref,
    visit_ref,
    home_ref,
    back_ref,
    home_got,
    back_got,
    t_ref,
    u_ref,
    local_sem,
    in_send,
    in_recv,
    home_send,
    home_recv,
    back_send,
    back_recv,
):
    own_count, _, plane = orbitals_ref.shape
    split_count = groups // own_count
    count = own_count // split_count
    planes = grid // groups
    per_set = bands_per_set(count)
    width = per_set * ROUNDS * grid
    lines = step // grid
    halves = width // LANES
    part = plane // PARTS
    group, band = lax.axis_index("grp"), lax.axis_index("band")
    band_row = group // split_count
    own_start = lax.rem(group, split_count) * count

    def device(by, along):
        return (lax.rem(group + by, groups), lax.rem(band + along + ring, ring))

    locals_ = [
        pltpu.make_async_copy(orbitals_ref.at[pl.ds(own_start, count)], own_ref, local_sem.at[0]),
        pltpu.make_async_copy(right_hbm, right_ref, local_sem.at[1]),
        pltpu.make_async_copy(slim_hbm, slim_ref, local_sem.at[2]),
        pltpu.make_async_copy(table_hbm, table_ref, local_sem.at[3]),
    ]
    for copy in locals_:
        copy.start()

    barrier = pltpu.get_barrier_semaphore()
    greeted = 0
    for along in range(-ROUNDS, ROUNDS + 1):
        for by in range(groups):
            if by or along:
                pl.semaphore_signal(
                    barrier, inc=1, device_id=device(by, along), device_id_type=MESH
                )
                greeted += 1
    pl.semaphore_wait(barrier, greeted)

    def remote(source, target, send, recv, where):
        copy = pltpu.make_async_remote_copy(
            src_ref=source,
            dst_ref=target,
            send_sem=send,
            recv_sem=recv,
            device_id=where,
            device_id_type=MESH,
        )
        copy.start()
        return copy

    def lanes_of(p):
        return pl.ds(p * part, part)

    def rows_of(by):
        return pl.ds(pl.multiple_of(lax.rem(group + by, groups) * planes, planes), planes)

    arrivals = [
        [
            remote(
                orbitals_ref.at[band_row, :, lanes_of(p)],
                visit_ref.at[d, :, lanes_of(p)],
                in_send.at[d, p],
                in_recv.at[d, p],
                device(0, d + 1),
            )
            for d in range(ROUNDS)
        ]
        for p in range(PARTS)
    ]

    def own_of(n, lanes):
        return own_ref[n, :, lanes].astype(jnp.float32)

    def slim_lines(values):
        return jnp.concatenate(
            [
                dot(slim_ref[...], parts_of(values[j * grid : (j + 1) * grid], 0))
                for j in range(lines)
            ],
            axis=0,
        )

    def forward(s, c, _):
        lanes = pl.ds(pl.multiple_of(c * step, step), step)
        visits = [visit_ref[d, :, lanes].astype(jnp.float32) for d in range(ROUNDS)]
        density = jnp.concatenate(
            [own_of(s * per_set + n, lanes) * v for n in range(per_set) for v in visits], axis=0
        )
        turned = dot(parts_of(density.T, 1), right_ref[...], ((1,), (1,)))
        turned = slim_lines(turned)
        for j in range(lines):
            for h in range(halves):
                t_ref[h, pl.ds(c * lines + j, grid, stride=grid), :] = turned[
                    j * grid : (j + 1) * grid, h * LANES : (h + 1) * LANES
                ]
        return 0

    def middle(k, _):
        for j in range(lines):
            row = k * lines + j
            rows = pl.ds(pl.multiple_of(row * grid, grid), grid)
            values = jnp.concatenate([t_ref[h, rows, :] for h in range(halves)], axis=1)
            scale = jnp.concatenate([table_ref[rows, :]] * halves, axis=1)
            values = dot(slim_ref[...], parts_of(values, 0)) * scale
            values = dot(slim_ref[...], parts_of(values, 0))
            for h in range(halves):
                u_ref[h, pl.ds(row, grid, stride=grid), :] = values[:, h * LANES : (h + 1) * LANES]
        return 0

    def backward(s, c, _):
        lanes = pl.ds(pl.multiple_of(c * step, step), step)
        values = jnp.concatenate([u_ref[h, lanes, :] for h in range(halves)], axis=1)
        values = slim_lines(values)
        potential = dot(right_ref[...], parts_of(values, 1), ((1,), (1,)))
        visits = [visit_ref[d, :, lanes].astype(jnp.float32) for d in range(ROUNDS)]
        totals = [back_ref[d, :, lanes] if s > 0 else None for d in range(ROUNDS)]
        for n in range(per_set):
            home = None
            own = own_of(s * per_set + n, lanes)
            for d in range(ROUNDS):
                pair = n * ROUNDS + d
                one = potential[pair * grid : (pair + 1) * grid, :]
                home = visits[d] * one if home is None else home + visits[d] * one
                totals[d] = own * one if totals[d] is None else totals[d] + own * one
            home_ref[s * per_set + n, :, lanes] = home
        for d in range(ROUNDS):
            back_ref[d, :, lanes] = totals[d]
        return 0

    chunks = part // step
    sets = count // per_set
    home_copies = [[[] for _ in range(PARTS)] for _ in range(sets)]
    back_copies = [[[] for _ in range(PARTS)] for _ in range(ROUNDS)]
    for copy in locals_:
        copy.wait()
    for s in range(sets):
        for p in range(PARTS):
            if s == 0:
                for d in range(ROUNDS):
                    arrivals[p][d].wait_recv()
            lax.fori_loop(
                p * chunks, (p + 1) * chunks, functools.partial(forward, s), 0, unroll=UNROLL
            )
        lax.fori_loop(0, grid // lines, middle, 0, unroll=UNROLL)
        for p in range(PARTS):
            lax.fori_loop(
                p * chunks, (p + 1) * chunks, functools.partial(backward, s), 0, unroll=UNROLL
            )
            lanes = lanes_of(p)
            if s == sets - 1:
                for d in range(ROUNDS):
                    for by in range(groups):
                        back_copies[d][p].append(
                            remote(
                                back_ref.at[d, rows_of(by), lanes],
                                back_got.at[d, by, :, lanes],
                                back_send.at[d, by, p],
                                back_recv.at[d, by, p],
                                device(by, -d - 1),
                            )
                        )
            members = pl.ds(s * per_set, per_set)
            for by in range(1, groups):
                home_copies[s][p].append(
                    remote(
                        home_ref.at[members, rows_of(by), lanes],
                        home_got.at[by - 1, members, :, lanes],
                        home_send.at[by - 1, s, p],
                        home_recv.at[by - 1, s, p],
                        device(by, 0),
                    )
                )

    if count < own_count:
        out_ref[...] = jnp.zeros_like(out_ref)
    out_ref[pl.ds(own_start, count)] = home_ref[:, rows_of(0), :]
    for s in range(sets):
        for p in range(PARTS):
            lanes = lanes_of(p)
            for by in range(1, groups):
                home_copies[s][p][by - 1].wait_recv()
                source = lax.rem(group + groups - by, groups)
                start = lax.rem(source, split_count) * count + s * per_set
                members = pl.ds(s * per_set, per_set)
                out_ref[pl.ds(start, per_set), :, lanes] += home_got[by - 1, members, :, lanes]
            if s == sets - 1:
                for d in range(ROUNDS):
                    for by in range(groups):
                        back_copies[d][p][by].wait_recv()
                        row = lax.rem(group + groups - by, groups) // split_count
                        out_ref[row, :, lanes] += back_got[d, by, :, lanes]
    for p in range(PARTS):
        for s in range(sets):
            for copy in home_copies[s][p]:
                copy.wait_send()
        for d in range(ROUNDS):
            arrivals[p][d].wait_send()
            for copy in back_copies[d][p]:
                copy.wait_send()


def body(orbitals):
    own_count, grid, plane = orbitals.shape
    groups, ring = lax.axis_size("grp"), lax.axis_size("band")
    count = own_count // (groups // own_count)
    planes = grid // groups
    per_set = bands_per_set(count)
    width = per_set * ROUNDS * grid
    step = 4 * grid
    table = kernel_table(grid).reshape(grid * grid, grid) * (-0.25 / float(grid**3))
    consts = (
        jnp.asarray(np.tile(table, (1, LANES // grid)).astype(np.float32)),
        jnp.asarray(tables(grid, per_set * ROUNDS)),
        jnp.asarray(tables(grid, 1)),
    )
    vmem = pl.BlockSpec(memory_space=pltpu.VMEM)
    dma = pltpu.SemaphoreType.DMA
    return pl.pallas_call(
        functools.partial(exchange_kernel, grid, step, groups, ring),
        out_shape=jax.ShapeDtypeStruct((own_count, planes, plane), jnp.float32),
        in_specs=[pl.BlockSpec(memory_space=pltpu.HBM)] * 4,
        out_specs=vmem,
        scratch_shapes=[
            pltpu.VMEM((count, grid, plane), jnp.bfloat16),
            *[pltpu.VMEM(c.shape, c.dtype) for c in consts],
            pltpu.VMEM((ROUNDS, grid, plane), jnp.bfloat16),
            pltpu.VMEM((count, grid, plane), jnp.float32),
            pltpu.VMEM((ROUNDS, grid, plane), jnp.float32),
            pltpu.VMEM((groups - 1, count, planes, plane), jnp.float32),
            pltpu.VMEM((ROUNDS, groups, planes, plane), jnp.float32),
            pltpu.VMEM((width // LANES, grid * grid, LANES), jnp.float32),
            pltpu.VMEM((width // LANES, grid * grid, LANES), jnp.float32),
            dma((4,)),
            dma((ROUNDS, PARTS)),
            dma((ROUNDS, PARTS)),
            dma((groups - 1, count // per_set, PARTS)),
            dma((groups - 1, count // per_set, PARTS)),
            dma((ROUNDS, groups, PARTS)),
            dma((ROUNDS, groups, PARTS)),
        ],
        compiler_params=pltpu.CompilerParams(
            collective_id=0, has_side_effects=True, vmem_limit_bytes=60 * 1024 * 1024
        ),
    )(orbitals, *consts)


def solution(mesh):
    return jax.shard_map(
        body,
        mesh=mesh,
        in_specs=(P("band", None, None),),
        out_specs=P("band", "grp", None),
        check_vma=False,
    )
```

```python
import functools
import math

import jax
import jax.numpy as jnp
import ml_dtypes
import numpy as np
from jax import lax
from jax.experimental import pallas as pl
from jax.experimental.pallas import tpu as pltpu
from jax.sharding import PartitionSpec as P

ROUNDS = 2


CELL_LENGTH = 41.05
SCREENING = 0.106
LANES = 128
PARTS = 4
UNROLL = 4
MESH = pl.DeviceIdType.MESH


def kernel_table(grid):
    wavenum = np.arange(grid, dtype=np.float64)
    wavenum = np.where(wavenum < grid // 2, wavenum, wavenum - grid) * (2.0 * math.pi / CELL_LENGTH)
    squared = (
        wavenum[:, None, None] ** 2 + wavenum[None, :, None] ** 2 + wavenum[None, None, :] ** 2
    )
    safe = np.where(squared > 0, squared, 1.0)
    screened = 4.0 * math.pi * (1.0 - np.exp(-safe / (4.0 * SCREENING * SCREENING))) / safe
    return np.where(squared > 0, screened, math.pi / (SCREENING * SCREENING))


def tables(grid, copies):
    indices = np.arange(grid)
    angles = (indices[:, None] * indices[None, :] % grid) * (2.0 * math.pi / grid)
    wide = np.kron(np.eye(copies), np.cos(angles) + np.sin(angles))
    high = wide.astype(ml_dtypes.bfloat16)
    low = (wide - high.astype(np.float64)).astype(ml_dtypes.bfloat16)
    return np.concatenate([high, high, low], axis=1)


def parts_of(values, axis):
    high = values.astype(jnp.bfloat16)
    low = (values - high.astype(jnp.float32)).astype(jnp.bfloat16)
    return jnp.concatenate([high, low, high], axis=axis)


def dot(a, b, dims=((1,), (0,))):
    return lax.dot_general(a, b, (dims, ((), ())), preferred_element_type=jnp.float32)


def exchange_kernel(
    grid,
    step,
    groups,
    ring,
    orbitals_ref,
    table_hbm,
    right_hbm,
    slim_hbm,
    out_ref,
    own_ref,
    table_ref,
    right_ref,
    slim_ref,
    visit_ref,
    home_ref,
    back_ref,
    home_got,
    back_got,
    t_ref,
    u_ref,
    local_sem,
    in_send,
    in_recv,
    home_send,
    home_recv,
    back_send,
    back_recv,
):
    own_count, _, plane = orbitals_ref.shape
    split_count = groups // own_count
    count = own_count // split_count
    planes = grid // groups
    width = count * grid
    lines = step // grid
    halves = width // LANES
    part = plane // PARTS
    group, band = lax.axis_index("grp"), lax.axis_index("band")
    band_row = group // split_count
    own_start = lax.rem(group, split_count) * count

    def device(by, along):
        return (lax.rem(group + by, groups), lax.rem(band + along + ring, ring))

    locals_ = [
        pltpu.make_async_copy(orbitals_ref.at[pl.ds(own_start, count)], own_ref, local_sem.at[0]),
        pltpu.make_async_copy(right_hbm, right_ref, local_sem.at[1]),
        pltpu.make_async_copy(slim_hbm, slim_ref, local_sem.at[2]),
        pltpu.make_async_copy(table_hbm, table_ref, local_sem.at[3]),
    ]
    for copy in locals_:
        copy.start()

    barrier = pltpu.get_barrier_semaphore()
    greeted = 0
    for along in range(-ROUNDS, ROUNDS + 1):
        for by in range(groups):
            if by or along:
                pl.semaphore_signal(
                    barrier, inc=1, device_id=device(by, along), device_id_type=MESH
                )
                greeted += 1
    pl.semaphore_wait(barrier, greeted)

    def remote(source, target, send, recv, where):
        copy = pltpu.make_async_remote_copy(
            src_ref=source,
            dst_ref=target,
            send_sem=send,
            recv_sem=recv,
            device_id=where,
            device_id_type=MESH,
        )
        copy.start()
        return copy

    def lanes_of(p):
        return pl.ds(p * part, part)

    def rows_of(by):
        return pl.ds(pl.multiple_of(lax.rem(group + by, groups) * planes, planes), planes)

    arrivals = [
        [
            remote(
                orbitals_ref.at[band_row, :, lanes_of(p)],
                visit_ref.at[d, :, lanes_of(p)],
                in_send.at[d, p],
                in_recv.at[d, p],
                device(0, d + 1),
            )
            for p in range(PARTS)
        ]
        for d in range(ROUNDS)
    ]

    def own_of(n, lanes):
        return own_ref[n, :, lanes].astype(jnp.float32)

    def slim_lines(values):
        return jnp.concatenate(
            [
                dot(slim_ref[...], parts_of(values[j * grid : (j + 1) * grid], 0))
                for j in range(lines)
            ],
            axis=0,
        )

    def forward(d, c, _):
        lanes = pl.ds(pl.multiple_of(c * step, step), step)
        visit = visit_ref[d, :, lanes].astype(jnp.float32)
        density = jnp.concatenate([own_of(n, lanes) * visit for n in range(count)], axis=0)
        turned = dot(parts_of(density.T, 1), right_ref[...], ((1,), (1,)))
        turned = slim_lines(turned)
        for j in range(lines):
            for h in range(halves):
                t_ref[h, pl.ds(c * lines + j, grid, stride=grid), :] = turned[
                    j * grid : (j + 1) * grid, h * LANES : (h + 1) * LANES
                ]
        return 0

    def middle(k, _):
        for j in range(lines):
            row = k * lines + j
            rows = pl.ds(pl.multiple_of(row * grid, grid), grid)
            values = jnp.concatenate([t_ref[h, rows, :] for h in range(halves)], axis=1)
            scale = jnp.concatenate([table_ref[rows, :]] * halves, axis=1)
            values = dot(slim_ref[...], parts_of(values, 0)) * scale
            values = dot(slim_ref[...], parts_of(values, 0))
            for h in range(halves):
                u_ref[h, pl.ds(row, grid, stride=grid), :] = values[:, h * LANES : (h + 1) * LANES]
        return 0

    def backward(d, c, _):
        lanes = pl.ds(pl.multiple_of(c * step, step), step)
        values = jnp.concatenate([u_ref[h, lanes, :] for h in range(halves)], axis=1)
        values = slim_lines(values)
        potential = dot(right_ref[...], parts_of(values, 1), ((1,), (1,)))
        visit = visit_ref[d, :, lanes].astype(jnp.float32)
        total = None
        for n in range(count):
            one = potential[n * grid : (n + 1) * grid, :]
            term = visit * one
            if d > 0:
                term = term + home_ref[n, :, lanes]
            home_ref[n, :, lanes] = term
            term = own_of(n, lanes) * one
            total = term if total is None else total + term
        back_ref[d, :, lanes] = total
        return 0

    chunks = part // step
    home_copies = [[] for _ in range(PARTS)]
    back_copies = [[[] for _ in range(PARTS)] for _ in range(ROUNDS)]
    for copy in locals_:
        copy.wait()
    for d in range(ROUNDS):
        for p in range(PARTS):
            arrivals[d][p].wait_recv()
            lax.fori_loop(p * chunks, (p + 1) * chunks, functools.partial(forward, d), 0, unroll=UNROLL)
        lax.fori_loop(0, grid // lines, middle, 0, unroll=UNROLL)
        for p in range(PARTS):
            lax.fori_loop(p * chunks, (p + 1) * chunks, functools.partial(backward, d), 0, unroll=UNROLL)
            lanes = lanes_of(p)
            for by in range(groups):
                back_copies[d][p].append(
                    remote(
                        back_ref.at[d, rows_of(by), lanes],
                        back_got.at[d, by, :, lanes],
                        back_send.at[d, by, p],
                        back_recv.at[d, by, p],
                        device(by, -d - 1),
                    )
                )
            if d == ROUNDS - 1:
                for by in range(1, groups):
                    home_copies[p].append(
                        remote(
                            home_ref.at[:, rows_of(by), lanes],
                            home_got.at[by - 1, :, :, lanes],
                            home_send.at[by - 1, p],
                            home_recv.at[by - 1, p],
                            device(by, 0),
                        )
                    )

    if count < own_count:
        out_ref[...] = jnp.zeros_like(out_ref)
    out_ref[pl.ds(own_start, count)] = home_ref[:, rows_of(0), :]
    for d in range(ROUNDS):
        for p in range(PARTS):
            lanes = lanes_of(p)
            if d == ROUNDS - 1:
                for by in range(1, groups):
                    home_copies[p][by - 1].wait_recv()
                    source = lax.rem(group + groups - by, groups)
                    start = lax.rem(source, split_count) * count
                    out_ref[pl.ds(start, count), :, lanes] += home_got[by - 1, :, :, lanes]
            for by in range(groups):
                back_copies[d][p][by].wait_recv()
                row = lax.rem(group + groups - by, groups) // split_count
                out_ref[row, :, lanes] += back_got[d, by, :, lanes]
    for p in range(PARTS):
        for copy in home_copies[p]:
            copy.wait_send()
        for d in range(ROUNDS):
            arrivals[d][p].wait_send()
            for copy in back_copies[d][p]:
                copy.wait_send()


def body(orbitals):
    own_count, grid, plane = orbitals.shape
    groups, ring = lax.axis_size("grp"), lax.axis_size("band")
    count = own_count // (groups // own_count)
    planes = grid // groups
    width = count * grid
    step = 4 * grid
    table = kernel_table(grid).reshape(grid * grid, grid) * (-0.25 / float(grid**3))
    consts = (
        jnp.asarray(np.tile(table, (1, LANES // grid)).astype(np.float32)),
        jnp.asarray(tables(grid, count)),
        jnp.asarray(tables(grid, 1)),
    )
    vmem = pl.BlockSpec(memory_space=pltpu.VMEM)
    dma = pltpu.SemaphoreType.DMA
    return pl.pallas_call(
        functools.partial(exchange_kernel, grid, step, groups, ring),
        out_shape=jax.ShapeDtypeStruct((own_count, planes, plane), jnp.float32),
        in_specs=[pl.BlockSpec(memory_space=pl.ANY)] * 4,
        out_specs=vmem,
        scratch_shapes=[
            pltpu.VMEM((count, grid, plane), jnp.bfloat16),
            *[pltpu.VMEM(c.shape, c.dtype) for c in consts],
            pltpu.VMEM((ROUNDS, grid, plane), jnp.bfloat16),
            pltpu.VMEM((count, grid, plane), jnp.float32),
            pltpu.VMEM((ROUNDS, grid, plane), jnp.float32),
            pltpu.VMEM((groups - 1, count, planes, plane), jnp.float32),
            pltpu.VMEM((ROUNDS, groups, planes, plane), jnp.float32),
            pltpu.VMEM((width // LANES, grid * grid, LANES), jnp.float32),
            pltpu.VMEM((width // LANES, grid * grid, LANES), jnp.float32),
            dma((4,)),
            dma((ROUNDS, PARTS)),
            dma((ROUNDS, PARTS)),
            dma((groups - 1, PARTS)),
            dma((groups - 1, PARTS)),
            dma((ROUNDS, groups, PARTS)),
            dma((ROUNDS, groups, PARTS)),
        ],
        compiler_params=pltpu.CompilerParams(
            collective_id=0, has_side_effects=True, vmem_limit_bytes=60 * 1024 * 1024
        ),
    )(orbitals, *consts)


def solution(mesh):
    return jax.shard_map(
        body,
        mesh=mesh,
        in_specs=(P("band", None, None),),
        out_specs=P("band", "grp", None),
        check_vma=False,
    )
```

```python
import functools
import math

import jax
import jax.numpy as jnp
import ml_dtypes
import numpy as np
from jax import lax
from jax.experimental import pallas as pl
from jax.experimental.pallas import tpu as pltpu
from jax.sharding import PartitionSpec as P

ROUNDS = 2


CELL_LENGTH = 41.05
SCREENING = 0.106
LANES = 128
PARTS = 4
UNROLL = 4
MESH = pl.DeviceIdType.MESH


def kernel_table(grid):
    wavenum = np.arange(grid, dtype=np.float64)
    wavenum = np.where(wavenum < grid // 2, wavenum, wavenum - grid) * (2.0 * math.pi / CELL_LENGTH)
    squared = (
        wavenum[:, None, None] ** 2 + wavenum[None, :, None] ** 2 + wavenum[None, None, :] ** 2
    )
    safe = np.where(squared > 0, squared, 1.0)
    screened = 4.0 * math.pi * (1.0 - np.exp(-safe / (4.0 * SCREENING * SCREENING))) / safe
    return np.where(squared > 0, screened, math.pi / (SCREENING * SCREENING))


def tables(grid, copies):
    indices = np.arange(grid)
    angles = (indices[:, None] * indices[None, :] % grid) * (2.0 * math.pi / grid)
    wide = np.kron(np.eye(copies), np.cos(angles) + np.sin(angles))
    high = wide.astype(ml_dtypes.bfloat16)
    low = (wide - high.astype(np.float64)).astype(ml_dtypes.bfloat16)
    return np.concatenate([high, high, low], axis=1)


def parts_of(values, axis):
    high = values.astype(jnp.bfloat16)
    low = (values - high.astype(jnp.float32)).astype(jnp.bfloat16)
    return jnp.concatenate([high, low, high], axis=axis)


def dot(a, b, dims=((1,), (0,))):
    return lax.dot_general(a, b, (dims, ((), ())), preferred_element_type=jnp.float32)


def exchange_kernel(
    grid,
    step,
    groups,
    ring,
    orbitals_ref,
    table_hbm,
    right_hbm,
    slim_hbm,
    kept_ref,
    out_ref,
    own_ref,
    table_ref,
    right_ref,
    slim_ref,
    visit_ref,
    home_ref,
    back_ref,
    home_got,
    back_got,
    t_ref,
    u_ref,
    local_sem,
    in_send,
    in_recv,
    home_send,
    home_recv,
    back_send,
    back_recv,
):
    own_count, _, plane = orbitals_ref.shape
    split_count = groups // own_count
    count = own_count // split_count
    planes = grid // groups
    width = count * grid
    lines = step // grid
    halves = width // LANES
    part = plane // PARTS
    group, band = lax.axis_index("grp"), lax.axis_index("band")
    band_row = group // split_count
    own_start = lax.rem(group, split_count) * count

    def device(by, along):
        return (lax.rem(group + by, groups), lax.rem(band + along + ring, ring))

    locals_ = [
        pltpu.make_async_copy(orbitals_ref.at[pl.ds(own_start, count)], own_ref, local_sem.at[0]),
        pltpu.make_async_copy(right_hbm, right_ref, local_sem.at[1]),
        pltpu.make_async_copy(slim_hbm, slim_ref, local_sem.at[2]),
        pltpu.make_async_copy(table_hbm, table_ref, local_sem.at[3]),
    ]
    for copy in locals_:
        copy.start()

    barrier = pltpu.get_barrier_semaphore()
    greeted = 0
    for along in range(-ROUNDS, ROUNDS + 1):
        for by in range(groups):
            if by or along:
                pl.semaphore_signal(
                    barrier, inc=1, device_id=device(by, along), device_id_type=MESH
                )
                greeted += 1
    pl.semaphore_wait(barrier, greeted)

    def remote(source, target, send, recv, where):
        copy = pltpu.make_async_remote_copy(
            src_ref=source,
            dst_ref=target,
            send_sem=send,
            recv_sem=recv,
            device_id=where,
            device_id_type=MESH,
        )
        copy.start()
        return copy

    def lanes_of(p):
        return pl.ds(p * part, part)

    def rows_of(by):
        return pl.ds(pl.multiple_of(lax.rem(group + by, groups) * planes, planes), planes)

    arrivals = [
        [
            remote(
                orbitals_ref.at[band_row, :, lanes_of(p)],
                visit_ref.at[d, :, lanes_of(p)],
                in_send.at[d, p],
                in_recv.at[d, p],
                device(0, d + 1),
            )
            for p in range(PARTS)
        ]
        for d in range(ROUNDS)
    ]

    def own_of(n, lanes):
        return own_ref[n, :, lanes].astype(jnp.float32)

    def slim_lines(values):
        return jnp.concatenate(
            [
                dot(slim_ref[...], parts_of(values[j * grid : (j + 1) * grid], 0))
                for j in range(lines)
            ],
            axis=0,
        )

    def forward(d, c, _):
        lanes = pl.ds(pl.multiple_of(c * step, step), step)
        visit = visit_ref[d, :, lanes].astype(jnp.float32)
        density = jnp.concatenate([own_of(n, lanes) * visit for n in range(count)], axis=0)
        turned = dot(parts_of(density.T, 1), right_ref[...], ((1,), (1,)))
        turned = slim_lines(turned)
        for j in range(lines):
            for h in range(halves):
                t_ref[h, pl.ds(c * lines + j, grid, stride=grid), :] = turned[
                    j * grid : (j + 1) * grid, h * LANES : (h + 1) * LANES
                ]
        return 0

    def middle(k, _):
        for j in range(lines):
            row = k * lines + j
            rows = pl.ds(pl.multiple_of(row * grid, grid), grid)
            values = jnp.concatenate([t_ref[h, rows, :] for h in range(halves)], axis=1)
            scale = jnp.concatenate([table_ref[rows, :]] * halves, axis=1)
            values = dot(slim_ref[...], parts_of(values, 0)) * scale
            values = dot(slim_ref[...], parts_of(values, 0))
            for h in range(halves):
                u_ref[h, pl.ds(row, grid, stride=grid), :] = values[:, h * LANES : (h + 1) * LANES]
        return 0

    def backward(d, c, _):
        lanes = pl.ds(pl.multiple_of(c * step, step), step)
        values = jnp.concatenate([u_ref[h, lanes, :] for h in range(halves)], axis=1)
        values = slim_lines(values)
        potential = dot(right_ref[...], parts_of(values, 1), ((1,), (1,)))
        visit = visit_ref[d, :, lanes].astype(jnp.float32)
        total = None
        for n in range(count):
            one = potential[n * grid : (n + 1) * grid, :]
            term = visit * one
            if d > 0:
                term = term + home_ref[n, :, lanes]
            home_ref[n, :, lanes] = term
            term = own_of(n, lanes) * one
            total = term if total is None else total + term
        back_ref[d, :, lanes] = total
        return 0

    chunks = part // step
    home_copies = [[] for _ in range(PARTS)]
    back_copies = [[[] for _ in range(PARTS)] for _ in range(ROUNDS)]
    for copy in locals_:
        copy.wait()
    for d in range(ROUNDS):
        for p in range(PARTS):
            arrivals[d][p].wait_recv()
            lax.fori_loop(p * chunks, (p + 1) * chunks, functools.partial(forward, d), 0, unroll=UNROLL)
        lax.fori_loop(0, grid // lines, middle, 0, unroll=UNROLL)
        for p in range(PARTS):
            lax.fori_loop(p * chunks, (p + 1) * chunks, functools.partial(backward, d), 0, unroll=UNROLL)
            lanes = lanes_of(p)
            for by in range(groups):
                back_copies[d][p].append(
                    remote(
                        back_ref.at[d, rows_of(by), lanes],
                        back_got.at[d, by, :, lanes],
                        back_send.at[d, by, p],
                        back_recv.at[d, by, p],
                        device(by, -d - 1),
                    )
                )
            if d == ROUNDS - 1:
                for by in range(1, groups):
                    home_copies[p].append(
                        remote(
                            home_ref.at[:, rows_of(by), lanes],
                            home_got.at[by - 1, :, :, lanes],
                            home_send.at[by - 1, p],
                            home_recv.at[by - 1, p],
                            device(by, 0),
                        )
                    )

    if count < own_count:
        kept_ref[...] = jnp.zeros_like(kept_ref)
    kept_ref[pl.ds(own_start, count)] = home_ref[:, rows_of(0), :]
    out_ref[...] = jnp.zeros_like(out_ref)
    for d in range(ROUNDS):
        for p in range(PARTS):
            lanes = lanes_of(p)
            if d == ROUNDS - 1:
                for by in range(1, groups):
                    home_copies[p][by - 1].wait_recv()
                    source = lax.rem(group + groups - by, groups)
                    start = lax.rem(source, split_count) * count
                    out_ref[pl.ds(start, count), :, lanes] += home_got[by - 1, :, :, lanes]
            for by in range(groups):
                back_copies[d][p][by].wait_recv()
                row = lax.rem(group + groups - by, groups) // split_count
                out_ref[row, :, lanes] += back_got[d, by, :, lanes]
    for p in range(PARTS):
        for copy in home_copies[p]:
            copy.wait_send()
        for d in range(ROUNDS):
            arrivals[d][p].wait_send()
            for copy in back_copies[d][p]:
                copy.wait_send()


def body(orbitals):
    own_count, grid, plane = orbitals.shape
    groups, ring = lax.axis_size("grp"), lax.axis_size("band")
    count = own_count // (groups // own_count)
    planes = grid // groups
    width = count * grid
    step = 4 * grid
    table = kernel_table(grid).reshape(grid * grid, grid) * (-0.25 / float(grid**3))
    consts = (
        jnp.asarray(np.tile(table, (1, LANES // grid)).astype(np.float32)),
        jnp.asarray(tables(grid, count)),
        jnp.asarray(tables(grid, 1)),
    )
    vmem = pl.BlockSpec(memory_space=pltpu.VMEM)
    dma = pltpu.SemaphoreType.DMA
    kept, received = pl.pallas_call(
        functools.partial(exchange_kernel, grid, step, groups, ring),
        out_shape=(jax.ShapeDtypeStruct((own_count, planes, plane), jnp.float32),) * 2,
        in_specs=[pl.BlockSpec(memory_space=pl.ANY)] * 4,
        out_specs=(vmem, vmem),
        scratch_shapes=[
            pltpu.VMEM((count, grid, plane), jnp.bfloat16),
            *[pltpu.VMEM(c.shape, c.dtype) for c in consts],
            pltpu.VMEM((ROUNDS, grid, plane), jnp.bfloat16),
            pltpu.VMEM((count, grid, plane), jnp.float32),
            pltpu.VMEM((ROUNDS, grid, plane), jnp.float32),
            pltpu.VMEM((groups - 1, count, planes, plane), jnp.float32),
            pltpu.VMEM((ROUNDS, groups, planes, plane), jnp.float32),
            pltpu.VMEM((width // LANES, grid * grid, LANES), jnp.float32),
            pltpu.VMEM((width // LANES, grid * grid, LANES), jnp.float32),
            dma((4,)),
            dma((ROUNDS, PARTS)),
            dma((ROUNDS, PARTS)),
            dma((groups - 1, PARTS)),
            dma((groups - 1, PARTS)),
            dma((ROUNDS, groups, PARTS)),
            dma((ROUNDS, groups, PARTS)),
        ],
        compiler_params=pltpu.CompilerParams(
            collective_id=0, has_side_effects=True, vmem_limit_bytes=60 * 1024 * 1024
        ),
    )(orbitals, *consts)
    return kept + received


def solution(mesh):
    return jax.shard_map(
        body,
        mesh=mesh,
        in_specs=(P("band", None, None),),
        out_specs=P("band", "grp", None),
        check_vma=False,
    )
```
